32 devices in a mesh: seq: 8 (over z, core), head: 4 (over y, x).
Axes of the slice: x: 2, y: 2, z: 4, core: 2. Of those that a mesh axis runs over, the one named last changes fastest.
Arguments:
- tokens: bfloat16 [2048, 4096], P('seq', 'head'), may hold values from -40 to 40
- norm_gain: float32 [4096], replicated, may hold values from 1.5 to 8
- w_qkv: bfloat16 [4096, 3, 512], P(None, None, 'head'), may hold values from -0.09375 to 0.09375
- w_out: bfloat16 [512, 4096], P('head'), may hold values from -0.75 to 0.75
- span_order: int32 [16], replicated, may hold values from 0 to 15, each once
- frame_id: int32 [2048], replicated, may hold values from 0 to 15, never falling along the last dimension, each value on 1 to 256 neighbouring positions
- camera_id: int32 [2048], replicated, may hold values from 0 to 5
Outputs:
- mixed: bfloat16 [2048, 4096], P('seq', 'head')
The draws below stay inside these ranges and needn't reach their ends.
Inputs may be any that keep to these rules, and one draw needn't show every extreme that they name: `span_order`: each of the 16 spans appears once. `frame_id`: never falls along the sequence; every frame has 1 to 256 positions and one has exactly 256.
All inputs are finite; a program needn't handle non-finite values.
Results may differ from the reference program's by a relative error of at most 0.015.
The reference program's roundings to bfloat16 on the way count: a program that leaves them out, or rounds other values in their place, can miss the bound.
Values may be sent and summed in bfloat16 or wider, within the bound.
A program may use at most 64 MiB of HBM per device.

```python
import math
import jax
import jax.numpy as jnp
import numpy as np
from jax import lax

D = 4096
HD = 128
HEADS = 4
TOK_DEV = 256
SEQ_LEN = 2048
SPANS = 16
FRAMES = 16
FRAME_MOST = 256
CAMERAS = 6
N_SEQ = 8


def draw_tokens(key, part):
    key_rows, key_cols, key_base = jax.random.split(jax.random.fold_in(key, 11), 3)
    row_scale = jnp.exp(jax.random.uniform(key_rows, (SEQ_LEN, 1), jnp.float32, math.log(0.3), math.log(3.0)))
    col_scale = jnp.exp(jax.random.uniform(key_cols, (1, D), jnp.float32, math.log(0.5), math.log(2.0)))
    base_values = jax.random.normal(key_base, (SEQ_LEN, D), jnp.float32)
    values = jnp.clip(base_values * row_scale * col_scale, -40.0, 40.0)
    return values.astype(jnp.bfloat16)


def draw_norm_gain(key, part):
    key_gain = jax.random.fold_in(key, 23)
    lower, upper = (math.log(1.5), math.log(3.0))
    return jnp.exp(jax.random.uniform(key_gain, (D,), jnp.float32, lower, upper))


def place_ends(result, stream_key, smallest, largest):
    place = [jax.random.randint(jax.random.fold_in(stream_key, axis), (), 0, length) for axis, length in enumerate(result.shape)]
    longest = result.shape.index(max(result.shape))
    neighbour = place[:longest] + [(place[longest] + 1) % result.shape[longest]] + place[longest + 1:]
    return result.at[tuple(place)].set(smallest).at[tuple(neighbour)].set(largest)


def strengthened(drawn, key, source, target, blocks, factor):
    owner, partner = [(jnp.arange(drawn.shape[axis_at]) // (drawn.shape[axis_at] // blocks)).reshape([-1 if axis == axis_at else 1 for axis in range(drawn.ndim)]) for axis_at in (source, target)]
    chosen = jax.random.permutation(key, blocks)[partner]
    strong = (owner == chosen) | (owner == (partner + blocks // 2) % blocks)
    return jnp.where(strong, factor * drawn, drawn)


def block_scale(stream_key, shape, pieces, least, high):
    factor_of, own = 1.0, jax.random.fold_in(stream_key, 6)
    for position, blocks in pieces:
        heights = jnp.exp(jax.random.uniform(jax.random.fold_in(own, position), (blocks,), jnp.float32, least / len(pieces), high / len(pieces)))
        factor_of = factor_of * jnp.repeat(heights, shape[position] // blocks).reshape([-1 if axis == position else 1 for axis in range(len(shape))])
    return factor_of


def profile(amount, total, reach, skew):
    weights = [(1 << 20) // math.isqrt(grade ** skew) + 1 for grade in range(2, amount + 1)]
    surplus, given = total - reach - (amount - 1), [1] * (amount - 1)
    while surplus > 0:
        candidates = [i for i in range(amount - 1) if given[i] < reach]
        whole, remaining = sum([weights[i] for i in candidates]), surplus
        for i in candidates:
            addition = min(reach - given[i], max(1, remaining * weights[i] // whole), surplus)
            given[i] = given[i] + addition
            surplus = surplus - addition
    return np.array([reach] + given)


def ragged(own_key, count, total, most, skew):
    if count == 2:
        one = jax.random.randint(own_key, (), max(1, total - most), min(most, total - 1) + 1)
        return jnp.stack([one, total - one])
    tallies = jnp.asarray(profile(count, total, most, skew), jnp.int32)
    twos = (count - 1) // 2
    donor, sink = tallies[1:1 + 2 * twos:2], tallies[2:2 + 2 * twos:2]
    room = jnp.minimum(donor - 1, most - sink)
    passed = jax.random.randint(jax.random.fold_in(own_key, 1), (twos,), 0, 1 << 20) % (room + 1)
    tallies = tallies.at[1:1 + 2 * twos:2].set(donor - passed).at[2:2 + 2 * twos:2].set(sink + passed)
    return tallies[jax.random.permutation(jax.random.fold_in(own_key, 2), count)]


def centred(rng, dims, deviation, bound, pieces=(), kind=jnp.bfloat16):
    gain = block_scale(rng, dims, pieces, -0.22, 0.18) if pieces else 1.0
    array = jax.random.normal(rng, dims, jnp.float32) * deviation * gain
    return jnp.minimum(jnp.maximum(array, -bound), bound).astype(kind)


def bell_draw_with(own_key, shape, scale, most, pieces, heavy, kind=jnp.bfloat16):
    entries = scale * jax.random.normal(own_key, shape, jnp.float32)
    if pieces:
        entries = entries * block_scale(own_key, shape, pieces, -0.22, 0.18)
    return jnp.clip(strengthened(entries, jax.random.fold_in(own_key, 3), *heavy), -most, most).astype(kind)


def setup_inputs(seed: int = 0) -> dict:
    seeds = jax.random.split(jax.random.key(seed), 8)
    return {
        "tokens": draw_tokens(jax.random.fold_in(seeds[7], 71), 0),
        "norm_gain": draw_norm_gain(jax.random.fold_in(seeds[7], 71), 0),
        "w_qkv": centred(seeds[2], (D, 3, HEADS * HD), D ** -0.5, 0.09375, ((2, 4),)),
        "w_out": bell_draw_with(seeds[3], (HEADS * HD, D), HD ** -0.5, 0.75, ((0, 4),), (0, 1, 4, 2.0)),
        "span_order": jax.random.permutation(seeds[4], SPANS).astype(jnp.int32),
        "frame_id": jnp.searchsorted(jnp.cumsum(ragged(seeds[5], FRAMES, SEQ_LEN, FRAME_MOST, 1)), jnp.arange(SEQ_LEN), side="right").astype(jnp.int32),
        "camera_id": place_ends(jax.random.randint(seeds[6], (SEQ_LEN,), 0, CAMERAS), jax.random.fold_in(seeds[6], 1), 0, CAMERAS - 1).astype(jnp.int32),
    }


epsilon = 1e-06

def stored_order(id_table, span_order):
    span_count = span_order.shape[0]
    return id_table.reshape(span_count, -1)[span_order].reshape(-1)

def visible_pairs(query_frames, query_cameras, key_frames, key_cameras):
    earlier = key_frames[None, :] < query_frames[:, None]
    same_view = (key_frames[None, :] == query_frames[:, None]) & (key_cameras[None, :] == query_cameras[:, None])
    return earlier | same_view

def reference(tokens, norm_gain, w_qkv, w_out, span_order, frame_id, camera_id):
    frames = stored_order(frame_id, span_order)
    cameras = stored_order(camera_id, span_order)
    widened = tokens.astype(jnp.float32)
    inverse = lax.rsqrt(lax.optimization_barrier(jnp.mean(widened * widened, axis=1, keepdims=True)) + epsilon)
    normed = (widened * inverse * norm_gain).astype(jnp.bfloat16)
    score_scale = HD ** (-0.5)

    def head_output(head_index, running):
        column_start = head_index.astype(jnp.int32) * HD
        columns = lax.dynamic_slice_in_dim(w_qkv, column_start, HD, 2).reshape(D, 3 * HD)
        projected = jnp.dot(normed, columns, preferred_element_type=jnp.float32).astype(jnp.bfloat16)
        queries = projected[:, :HD]
        key_rows = projected[:, HD:2 * HD]
        value_rows = projected[:, 2 * HD:]

        def query_block(block_index):
            first_row = block_index.astype(jnp.int32) * TOK_DEV
            block_queries = lax.dynamic_slice_in_dim(queries, first_row, TOK_DEV, 0)
            block_frames = lax.dynamic_slice_in_dim(frames, first_row, TOK_DEV, 0)
            block_cameras = lax.dynamic_slice_in_dim(cameras, first_row, TOK_DEV, 0)
            scores = jnp.dot(block_queries, key_rows.T, preferred_element_type=jnp.float32) * score_scale
            allowed = visible_pairs(block_frames, block_cameras, frames, cameras)
            row_best = lax.optimization_barrier(jnp.max(jnp.where(allowed, scores, -jnp.inf), axis=1, keepdims=True))
            weights = jnp.exp(jnp.where(allowed, scores - row_best, -jnp.inf))
            weight_sum = lax.optimization_barrier(jnp.sum(weights, axis=1, keepdims=True))
            weighted = jnp.dot(weights.astype(jnp.bfloat16), value_rows, preferred_element_type=jnp.float32)
            return (weighted / weight_sum).astype(jnp.bfloat16)
        attended = lax.map(query_block, jnp.arange(N_SEQ, dtype=jnp.int32)).reshape(SEQ_LEN, HD)
        out_rows = lax.dynamic_slice_in_dim(w_out, column_start, HD, 0)
        head_part = jnp.dot(attended, out_rows, preferred_element_type=jnp.float32).astype(jnp.bfloat16)
        head_part = lax.optimization_barrier(head_part)
        return running + head_part.astype(jnp.float32)
    summed = lax.fori_loop(0, HEADS, head_output, jnp.zeros((SEQ_LEN, D), jnp.float32))
    return summed.astype(jnp.bfloat16)
```

```python
import functools
import math

import jax
import jax.numpy as jnp
from jax import lax
from jax.experimental import pallas as pl
from jax.experimental.pallas import tpu as pltpu
from jax.sharding import PartitionSpec as P

HD = 128
EPSILON = 1e-06
CHUNKS = 4
CODE = 1024
MESH = pl.DeviceIdType.MESH


def kernel(
    n_seq, n_head, tokens, gain, w_qkv, w_out, spans, frames, cameras, out,
    gathered, w_vmem, codes, queries, kv, w_all, att, acc, run_m, run_l, run_o,
    local_sem, t_send, t_recv, f_send, k_send, k_recv, r_send, w_send, w_recv, v_send, a_send, a_recv,
):
    seq, head = lax.axis_index("seq"), lax.axis_index("head")
    rows, width = tokens.shape
    half = width // 2
    part = rows // CHUNKS
    minor_n = n_head // max(k for k in range(1, math.isqrt(n_head) + 1) if n_head % k == 0)
    major_n = n_head // minor_n
    major, minor = head // minor_n, lax.rem(head, minor_n)
    core, layer = lax.rem(seq, 2), seq // 2
    layers = n_seq // 2
    sibling = layer * 2 + 1 - core
    minor_peers = [major * minor_n + lax.rem(minor + k, minor_n) for k in range(1, minor_n)]
    major_peers = [lax.rem(major + k, major_n) * minor_n + minor for k in range(1, major_n)]
    far_peers = [
        lax.rem(major + i, major_n) * minor_n + lax.rem(minor + k, minor_n)
        for i in range(1, major_n) for k in range(1, minor_n)
    ]
    head_peers = minor_peers + major_peers + far_peers
    layer_peers = [lax.rem(layer + k, layers) * 2 + core for k in range(1, layers)]
    sent = []

    def send(src, dst, send_sem, recv_sem, device):
        copy = pltpu.make_async_remote_copy(
            src_ref=src, dst_ref=dst, send_sem=send_sem, recv_sem=recv_sem,
            device_id=device, device_id_type=MESH,
        )
        copy.start()
        sent.append(copy)

    def arrived(dst, recv_sem):
        pltpu.make_async_remote_copy(
            src_ref=dst, dst_ref=dst, send_sem=recv_sem, recv_sem=recv_sem,
            device_id={"seq": sibling}, device_id_type=MESH,
        ).wait_recv()

    def token_slot(c, j, origin):
        column = pl.multiple_of(origin * width + j * half, 128)
        return gathered.at[pl.ds(c * part, part), pl.ds(column, half)]

    def kv_slot(c, origin):
        return kv.at[c, pl.ds(pl.multiple_of(origin * part, part), part), :]

    def w_slot(origin, j):
        first = pl.multiple_of(origin * HD + j * (HD // 2), HD // 2)
        return w_all.at[pl.ds(first, HD // 2), :]

    def own_tokens(c):
        for j in range(2):
            src = tokens.at[pl.ds(c * part, part), pl.ds(j * half, half)]
            near = minor_peers + major_peers if j == 0 else major_peers + minor_peers
            for i, peer in enumerate(near):
                send(src, token_slot(c, j, head), t_send.at[c, j, i], t_recv.at[c, j, head], {"head": peer})

    def forward_tokens(c):
        for j, (sources, targets) in enumerate(((minor_peers, major_peers), (major_peers, minor_peers))):
            for i, origin in enumerate(sources):
                slot = token_slot(c, j, origin)
                arrived(slot, t_recv.at[c, j, origin])
                for k, peer in enumerate(targets):
                    send(slot, slot, f_send.at[c, j, i * len(targets) + k], t_recv.at[c, j, origin], {"head": peer})

    def project(c):
        for j, late in enumerate((major_peers + far_peers, minor_peers + far_peers)):
            for origin in late:
                arrived(token_slot(c, j, origin), t_recv.at[c, j, origin])
        here = pl.ds(c * part, part)
        wide = gathered[here, :].astype(jnp.float32)
        inverse = lax.rsqrt(jnp.mean(wide * wide, axis=1, keepdims=True) + EPSILON)
        normed = (wide * inverse * gain[...]).astype(jnp.bfloat16)
        projected = jnp.dot(normed, w_vmem[...], preferred_element_type=jnp.float32).astype(jnp.bfloat16)
        queries[here, :] = projected[:, :HD]
        slot = kv_slot(c, seq)
        slot[...] = projected[:, HD:]
        for i, peer in enumerate(layer_peers):
            send(slot, slot, k_send.at[c, i], k_recv.at[c, seq], {"seq": peer})
        send(slot, slot, k_send.at[c, layers - 1], k_recv.at[c, seq], {"seq": sibling})

    def relay(c):
        for i, origin in enumerate(layer_peers):
            slot = kv_slot(c, origin)
            arrived(slot, k_recv.at[c, origin])
            send(slot, slot, r_send.at[c, i], k_recv.at[c, origin], {"seq": sibling})

    def others(c):
        for k in range(layers):
            origin = lax.rem(layer + k, layers) * 2 + 1 - core
            arrived(kv_slot(c, origin), k_recv.at[c, origin])

    barrier = pltpu.get_barrier_semaphore()
    for peer in head_peers:
        pl.semaphore_signal(barrier, inc=1, device_id={"head": peer}, device_id_type=MESH)
    for peer in layer_peers + [sibling]:
        pl.semaphore_signal(barrier, inc=1, device_id={"seq": peer}, device_id_type=MESH)
    pl.semaphore_wait(barrier, len(head_peers) + len(layer_peers) + 1)

    own_tokens(0)
    own_tokens(1)
    local = [
        pltpu.make_async_copy(w_qkv.at[j], w_vmem.at[:, pl.ds(j * HD, HD)], local_sem.at[j]) for j in range(3)
    ]
    local.append(pltpu.make_async_copy(
        tokens, gathered.at[:, pl.ds(pl.multiple_of(head * width, 128), width)], local_sem.at[3]))
    local.append(pltpu.make_async_copy(
        w_out.at[:, pl.ds(pl.multiple_of(head * width, 128), width)],
        w_all.at[pl.ds(pl.multiple_of(head * HD, HD), HD), :], local_sem.at[4]))
    for copy in local:
        copy.start()

    span_count, span = frames.shape
    for s in range(span_count):
        place = spans[s]
        codes[pl.ds(s, 1), :] = frames[pl.ds(place, 1), :] * CODE + cameras[pl.ds(place, 1), :]
    own_spans = rows // span
    query_codes = jnp.concatenate([
        jnp.broadcast_to(codes[pl.ds(seq * own_spans + i, 1), :], (HD, span)).T for i in range(own_spans)
    ], axis=0)[:, :1]
    query_bases = query_codes - jnp.bitwise_and(query_codes, CODE - 1)
    for copy in local:
        copy.wait()

    for c in range(CHUNKS):
        forward_tokens(c)
        if c + 2 < CHUNKS:
            own_tokens(c + 2)
        if c + 1 == CHUNKS:
            for i, peer in enumerate(head_peers):
                src = w_out.at[pl.ds(pl.multiple_of(core * (HD // 2), HD // 2), HD // 2),
                               pl.ds(pl.multiple_of(peer * width, 128), width)]
                send(src, w_slot(head, core), w_send.at[i], w_recv.at[head, core], {"head": peer})
        if c >= 1:
            project(c - 1)
        if c >= 2:
            relay(c - 2)
    project(CHUNKS - 1)
    relay(CHUNKS - 2)

    scale = HD ** -0.5
    run_m[...] = jnp.full(run_m.shape, -1e30, jnp.float32)
    run_l[...] = jnp.zeros(run_l.shape, jnp.float32)
    run_o[...] = jnp.zeros(run_o.shape, jnp.float32)

    def absorb(c):
        pieces = []
        for d in range(n_seq):
            first = d * rows + c * part
            lane = first % span
            pieces.append(codes[first // span:first // span + 1, lane:lane + part])
        key_codes = jnp.concatenate(pieces, axis=1)
        allowed = (key_codes == query_codes) | (key_codes < query_bases)
        scores = lax.dot_general(
            queries[...], kv[c, :, :HD], (((1,), (1,)), ((), ())), preferred_element_type=jnp.float32
        ) * scale
        scores = jnp.where(allowed, scores, -jnp.inf)
        old = run_m[...]
        best = jnp.maximum(old, jnp.max(scores, axis=1, keepdims=True))
        weights = jnp.exp(scores - best)
        factor = jnp.exp(old - best)
        run_m[...] = best
        run_l[...] = run_l[...] * factor + jnp.sum(weights, axis=1, keepdims=True)
        run_o[...] = run_o[...] * factor + jnp.dot(
            weights.astype(jnp.bfloat16), kv[c, :, HD:], preferred_element_type=jnp.float32)

    for c in range(CHUNKS - 1):
        others(c)
        absorb(c)
    relay(CHUNKS - 1)
    for i, origin in enumerate(head_peers):
        slot = w_slot(origin, core)
        arrived(slot, w_recv.at[origin, core])
        send(slot, slot, v_send.at[i], w_recv.at[origin, core], {"seq": sibling})
    others(CHUNKS - 1)
    absorb(CHUNKS - 1)
    att[head] = (run_o[...] / run_l[...]).astype(jnp.bfloat16)
    for i, peer in enumerate(head_peers):
        send(att.at[head], att.at[head], a_send.at[i], a_recv.at[head], {"head": peer})

    def head_out(origin):
        w_rows = w_all[pl.ds(pl.multiple_of(origin * HD, HD), HD), :]
        return jnp.dot(att[origin], w_rows, preferred_element_type=jnp.float32).astype(jnp.bfloat16).astype(jnp.float32)

    acc[...] = head_out(head)
    for i, origin in enumerate(head_peers):
        arrived(w_slot(origin, 1 - core), w_recv.at[origin, 1 - core])
        arrived(att.at[origin], a_recv.at[origin])
        if i + 1 < len(head_peers):
            acc[...] += head_out(origin)
        else:
            out[...] = (acc[...] + head_out(origin)).astype(jnp.bfloat16)
    for copy in sent:
        copy.wait_send()


def on_device(n_seq, n_head, tokens, norm_gain, w_qkv, w_out, span_order, frame_id, camera_id):
    rows, width = tokens.shape
    depth = norm_gain.shape[0]
    part = rows // CHUNKS
    spans = span_order.shape[0]
    vmem, smem, hbm = (pl.BlockSpec(memory_space=m) for m in (pltpu.VMEM, pltpu.SMEM, pl.ANY))
    dma = pltpu.SemaphoreType.DMA
    keys = n_seq * rows
    return pl.pallas_call(
        functools.partial(kernel, n_seq, n_head),
        out_shape=jax.ShapeDtypeStruct((rows, width), jnp.bfloat16),
        in_specs=[hbm, vmem, hbm, hbm, smem, vmem, vmem],
        out_specs=vmem,
        scratch_shapes=[
            pltpu.VMEM((rows, depth), jnp.bfloat16),
            pltpu.VMEM((depth, 3 * HD), jnp.bfloat16),
            pltpu.VMEM((spans, keys // spans), jnp.int32),
            pltpu.VMEM((rows, HD), jnp.bfloat16),
            pltpu.VMEM((CHUNKS, n_seq * part, 2 * HD), jnp.bfloat16),
            pltpu.VMEM((n_head * HD, width), jnp.bfloat16),
            pltpu.VMEM((n_head, rows, HD), jnp.bfloat16),
            pltpu.VMEM((rows, width), jnp.float32),
            pltpu.VMEM((rows, 1), jnp.float32),
            pltpu.VMEM((rows, 1), jnp.float32),
            pltpu.VMEM((rows, HD), jnp.float32),
            dma((5,)),
            dma((CHUNKS, 2, n_head)),
            dma((CHUNKS, 2, n_head)),
            dma((CHUNKS, 2, n_head)),
            dma((CHUNKS, n_seq // 2)),
            dma((CHUNKS, n_seq)),
            dma((CHUNKS, n_seq // 2)),
            dma((n_head,)),
            dma((n_head, 2)),
            dma((n_head,)),
            dma((n_head,)),
            dma((n_head,)),
        ],
        compiler_params=pltpu.CompilerParams(
            collective_id=0, has_side_effects=True, vmem_limit_bytes=48 * 1024 * 1024
        ),
    )(
        tokens, norm_gain.reshape(1, depth), w_qkv.transpose(1, 0, 2), w_out, span_order,
        frame_id.reshape(spans, -1), camera_id.reshape(spans, -1),
    )


def solution(mesh):
    placed = (P("seq", "head"), P(), P(None, None, "head"), P("head", None), P(), P(), P())
    body = functools.partial(on_device, mesh.shape["seq"], mesh.shape["head"])
    return jax.shard_map(body, mesh=mesh, in_specs=placed, out_specs=P("seq", "head"), check_vma=False)
```

```python
import functools
import math

import jax
import jax.numpy as jnp
from jax import lax
from jax.experimental import pallas as pl
from jax.experimental.pallas import tpu as pltpu
from jax.sharding import PartitionSpec as P

HD = 128
EPSILON = 1e-06
SHARES = (1, 1, 1, 1)
CHUNKS = len(SHARES)
CODE = 1024
MESH = pl.DeviceIdType.MESH


def kernel(
    n_seq, n_head, tokens, gain_in, w_qkv, w_out, spans_in, frames_in, cameras_in, out,
    gain, spans, frames, cameras, gathered, w_vmem, codes, queries, kv, w_all, att, acc, run_m, run_l, run_o,
    local_sem, t_send, t_recv, f_send, k_send, k_recv, r_send, w_send, w_recv, v_send, a_send, a_recv,
):
    seq, head = lax.axis_index("seq"), lax.axis_index("head")
    rows, width = tokens.shape
    half = width // 2
    sizes = [rows * share // sum(SHARES) for share in SHARES]
    starts = [sum(sizes[:c]) for c in range(CHUNKS)]
    minor_n = n_head // max(k for k in range(1, math.isqrt(n_head) + 1) if n_head % k == 0)
    major_n = n_head // minor_n
    major, minor = head // minor_n, lax.rem(head, minor_n)
    core, layer = lax.rem(seq, 2), seq // 2
    layers = n_seq // 2
    sibling = layer * 2 + 1 - core
    minor_peers = [major * minor_n + lax.rem(minor + k, minor_n) for k in range(1, minor_n)]
    major_peers = [lax.rem(major + k, major_n) * minor_n + minor for k in range(1, major_n)]
    far_peers = [
        lax.rem(major + i, major_n) * minor_n + lax.rem(minor + k, minor_n)
        for i in range(1, major_n) for k in range(1, minor_n)
    ]
    head_peers = minor_peers + major_peers + far_peers
    layer_peers = [lax.rem(layer + k, layers) * 2 + core for k in range(1, layers)]
    sent = []

    def send(src, dst, send_sem, recv_sem, device):
        copy = pltpu.make_async_remote_copy(
            src_ref=src, dst_ref=dst, send_sem=send_sem, recv_sem=recv_sem,
            device_id=device, device_id_type=MESH,
        )
        copy.start()
        sent.append(copy)

    def arrived(dst, recv_sem):
        pltpu.make_async_remote_copy(
            src_ref=dst, dst_ref=dst, send_sem=recv_sem, recv_sem=recv_sem,
            device_id={"seq": sibling}, device_id_type=MESH,
        ).wait_recv()

    def token_slot(c, j, origin):
        column = pl.multiple_of(origin * width + j * half, 128)
        return gathered.at[pl.ds(starts[c], sizes[c]), pl.ds(column, half)]

    def kv_slot(c, origin):
        first = pl.multiple_of(n_seq * starts[c] + origin * sizes[c], 16)
        return kv.at[pl.ds(first, sizes[c]), :]

    def w_slot(origin, j):
        first = pl.multiple_of(origin * HD + j * (HD // 2), HD // 2)
        return w_all.at[pl.ds(first, HD // 2), :]

    def own_tokens(c):
        for j in range(2):
            src = tokens.at[pl.ds(starts[c], sizes[c]), pl.ds(j * half, half)]
            near = minor_peers + major_peers if j == 0 else major_peers + minor_peers
            for i, peer in enumerate(near):
                send(src, token_slot(c, j, head), t_send.at[c, j, i], t_recv.at[c, j, head], {"head": peer})

    def forward_tokens(c):
        for j, (sources, targets) in enumerate(((minor_peers, major_peers), (major_peers, minor_peers))):
            for i, origin in enumerate(sources):
                slot = token_slot(c, j, origin)
                arrived(slot, t_recv.at[c, j, origin])
                for k, peer in enumerate(targets):
                    send(slot, slot, f_send.at[c, j, i * len(targets) + k], t_recv.at[c, j, origin], {"head": peer})

    def project(c):
        for j, late in enumerate((major_peers + far_peers, minor_peers + far_peers)):
            for origin in late:
                arrived(token_slot(c, j, origin), t_recv.at[c, j, origin])
        here = pl.ds(starts[c], sizes[c])
        wide = gathered[here, :].astype(jnp.float32)
        inverse = lax.rsqrt(jnp.mean(wide * wide, axis=1, keepdims=True) + EPSILON)
        normed = (wide * inverse * gain[...]).astype(jnp.bfloat16)
        projected = jnp.dot(normed, w_vmem[...], preferred_element_type=jnp.float32).astype(jnp.bfloat16)
        queries[here, :] = projected[:, :HD]
        slot = kv_slot(c, seq)
        slot[...] = projected[:, HD:]
        for i, peer in enumerate(layer_peers):
            send(slot, slot, k_send.at[c, i], k_recv.at[c, seq], {"seq": peer})
        send(slot, slot, k_send.at[c, layers - 1], k_recv.at[c, seq], {"seq": sibling})

    def relay(c):
        for i, origin in enumerate(layer_peers):
            slot = kv_slot(c, origin)
            arrived(slot, k_recv.at[c, origin])
            send(slot, slot, r_send.at[c, i], k_recv.at[c, origin], {"seq": sibling})

    def others(c):
        for k in range(layers):
            origin = lax.rem(layer + k, layers) * 2 + 1 - core
            arrived(kv_slot(c, origin), k_recv.at[c, origin])

    barrier = pltpu.get_barrier_semaphore()
    for peer in head_peers:
        pl.semaphore_signal(barrier, inc=1, device_id={"head": peer}, device_id_type=MESH)
    for peer in layer_peers + [sibling]:
        pl.semaphore_signal(barrier, inc=1, device_id={"seq": peer}, device_id_type=MESH)
    local = [
        pltpu.make_async_copy(w_qkv.at[j], w_vmem.at[:, pl.ds(j * HD, HD)], local_sem.at[j]) for j in range(3)
    ]
    local.append(pltpu.make_async_copy(
        tokens, gathered.at[:, pl.ds(pl.multiple_of(head * width, 128), width)], local_sem.at[3]))
    local.append(pltpu.make_async_copy(
        w_out.at[:, pl.ds(pl.multiple_of(head * width, 128), width)],
        w_all.at[pl.ds(pl.multiple_of(head * HD, HD), HD), :], local_sem.at[4]))
    small = [
        pltpu.make_async_copy(src, dst, local_sem.at[5 + i])
        for i, (src, dst) in enumerate(((spans_in, spans), (frames_in, frames), (cameras_in, cameras), (gain_in, gain)))
    ]
    for copy in small + local:
        copy.start()
    pl.semaphore_wait(barrier, len(head_peers) + len(layer_peers) + 1)

    own_tokens(0)
    own_tokens(1)
    for copy in small:
        copy.wait()

    span_count, span = frames.shape
    for s in range(span_count):
        place = spans[s]
        codes[pl.ds(s, 1), :] = frames[pl.ds(place, 1), :] * CODE + cameras[pl.ds(place, 1), :]
    own_spans = rows // span
    query_codes = jnp.concatenate([
        jnp.broadcast_to(codes[pl.ds(seq * own_spans + i, 1), :], (HD, span)).T for i in range(own_spans)
    ], axis=0)[:, :1]
    query_bases = query_codes - jnp.bitwise_and(query_codes, CODE - 1)
    for c in range(CHUNKS):
        forward_tokens(c)
        if c + 2 < CHUNKS:
            own_tokens(c + 2)
        if c + 1 == CHUNKS:
            for i, peer in enumerate(head_peers):
                src = w_out.at[pl.ds(pl.multiple_of(core * (HD // 2), HD // 2), HD // 2),
                               pl.ds(pl.multiple_of(peer * width, 128), width)]
                send(src, w_slot(head, core), w_send.at[i], w_recv.at[head, core], {"head": peer})
        if c == 1:
            for copy in local:
                copy.wait()
        if c >= 1:
            project(c - 1)
        if c >= 2:
            relay(c - 2)
    project(CHUNKS - 1)
    relay(CHUNKS - 2)

    scale = HD ** -0.5
    run_m[...] = jnp.full(run_m.shape, -1e30, jnp.float32)
    run_l[...] = jnp.zeros(run_l.shape, jnp.float32)
    run_o[...] = jnp.zeros(run_o.shape, jnp.float32)

    def absorb(c):
        pieces = []
        for d in range(n_seq):
            first, end = d * rows + starts[c], d * rows + starts[c] + sizes[c]
            while first < end:
                lane = first % span
                count = min(end - first, span - lane)
                pieces.append(codes[first // span:first // span + 1, lane:lane + count])
                first += count
        here = pl.ds(n_seq * starts[c], n_seq * sizes[c])
        key_codes = jnp.concatenate(pieces, axis=1)
        allowed = (key_codes == query_codes) | (key_codes < query_bases)
        scores = lax.dot_general(
            queries[...], kv[here, :HD], (((1,), (1,)), ((), ())), preferred_element_type=jnp.float32
        ) * scale
        scores = jnp.where(allowed, scores, -jnp.inf)
        old = run_m[...]
        best = jnp.maximum(old, jnp.max(scores, axis=1, keepdims=True))
        weights = jnp.exp(scores - best)
        factor = jnp.exp(old - best)
        run_m[...] = best
        run_l[...] = run_l[...] * factor + jnp.sum(weights, axis=1, keepdims=True)
        run_o[...] = run_o[...] * factor + jnp.dot(
            weights.astype(jnp.bfloat16), kv[here, HD:], preferred_element_type=jnp.float32)

    for c in range(CHUNKS - 1):
        others(c)
        absorb(c)
    relay(CHUNKS - 1)
    others(CHUNKS - 1)
    absorb(CHUNKS - 1)
    att[head] = (run_o[...] / run_l[...]).astype(jnp.bfloat16)
    for i, peer in enumerate(head_peers):
        send(att.at[head], att.at[head], a_send.at[i], a_recv.at[head], {"head": peer})
    for i, origin in enumerate(head_peers):
        slot = w_slot(origin, core)
        arrived(slot, w_recv.at[origin, core])
        send(slot, slot, v_send.at[i], w_recv.at[origin, core], {"seq": sibling})

    def head_out(origin):
        w_rows = w_all[pl.ds(pl.multiple_of(origin * HD, HD), HD), :]
        return jnp.dot(att[origin], w_rows, preferred_element_type=jnp.float32).astype(jnp.bfloat16).astype(jnp.float32)

    acc[...] = head_out(head)
    for i, origin in enumerate(head_peers):
        arrived(w_slot(origin, 1 - core), w_recv.at[origin, 1 - core])
        arrived(att.at[origin], a_recv.at[origin])
        if i + 1 < len(head_peers):
            acc[...] += head_out(origin)
        else:
            out[...] = (acc[...] + head_out(origin)).astype(jnp.bfloat16)
    for copy in sent:
        copy.wait_send()


def on_device(n_seq, n_head, tokens, norm_gain, w_qkv, w_out, span_order, frame_id, camera_id):
    rows, width = tokens.shape
    depth = norm_gain.shape[0]
    spans = span_order.shape[0]
    hbm = pl.BlockSpec(memory_space=pltpu.HBM)
    dma = pltpu.SemaphoreType.DMA
    keys = n_seq * rows
    return pl.pallas_call(
        functools.partial(kernel, n_seq, n_head),
        out_shape=jax.ShapeDtypeStruct((rows, width), jnp.bfloat16),
        in_specs=[hbm] * 7,
        out_specs=pl.BlockSpec(memory_space=pltpu.VMEM),
        scratch_shapes=[
            pltpu.VMEM((1, depth), jnp.float32),
            pltpu.SMEM((spans,), jnp.int32),
            pltpu.VMEM((spans, keys // spans), jnp.int32),
            pltpu.VMEM((spans, keys // spans), jnp.int32),
            pltpu.VMEM((rows, depth), jnp.bfloat16),
            pltpu.VMEM((depth, 3 * HD), jnp.bfloat16),
            pltpu.VMEM((spans, keys // spans), jnp.int32),
            pltpu.VMEM((rows, HD), jnp.bfloat16),
            pltpu.VMEM((keys, 2 * HD), jnp.bfloat16),
            pltpu.VMEM((n_head * HD, width), jnp.bfloat16),
            pltpu.VMEM((n_head, rows, HD), jnp.bfloat16),
            pltpu.VMEM((rows, width), jnp.float32),
            pltpu.VMEM((rows, 1), jnp.float32),
            pltpu.VMEM((rows, 1), jnp.float32),
            pltpu.VMEM((rows, HD), jnp.float32),
            dma((9,)),
            dma((CHUNKS, 2, n_head)),
            dma((CHUNKS, 2, n_head)),
            dma((CHUNKS, 2, n_head)),
            dma((CHUNKS, n_seq // 2)),
            dma((CHUNKS, n_seq)),
            dma((CHUNKS, n_seq // 2)),
            dma((n_head,)),
            dma((n_head, 2)),
            dma((n_head,)),
            dma((n_head,)),
            dma((n_head,)),
        ],
        compiler_params=pltpu.CompilerParams(
            collective_id=0, has_side_effects=True, vmem_limit_bytes=60 * 1024 * 1024
        ),
    )(
        tokens, norm_gain.reshape(1, depth), w_qkv.transpose(1, 0, 2), w_out, span_order,
        frame_id.reshape(spans, -1), camera_id.reshape(spans, -1),
    )


def solution(mesh):
    placed = (P("seq", "head"), P(), P(None, None, "head"), P("head", None), P(), P(), P())
    body = functools.partial(on_device, mesh.shape["seq"], mesh.shape["head"])
    return jax.shard_map(body, mesh=mesh, in_specs=placed, out_specs=P("seq", "head"), check_vma=False)
```
